32 devices in a mesh: dp: 4 (over z), mp: 8 (over y, x, core).
Axes of the slice: x: 2, y: 2, z: 4, core: 2. Of those that a mesh axis runs over, the one named last changes fastest.
Arguments:
- node_feats: bfloat16 [65536, 128], P(('dp', 'mp')), may hold values from -6 to 6
- batch_deg: int32 [65536], P(('dp', 'mp')), may hold values from 1 to 8
- batch_nbrs: int32 [65536, 8], P(('dp', 'mp')), may hold values from 0 to 2047
- halo_nbrs: int32 [65536, 8], P(('dp', 'mp')), may hold values from 0 to 511
- halo_len: int32 [65536], P(('dp', 'mp')), may hold values from 1 to 8
- halo_rows: int32 [16384], P(('dp', 'mp')), may hold values from 0 to 65535, as said below
- halo_deg: int32 [16384], P(('dp', 'mp')), may hold values from 1 to 8
- feat_table: bfloat16 [65536, 128], P(('dp', 'mp')), may hold values from -6 to 6
- emb_table: bfloat16 [65536, 512], P(('dp', 'mp')), may hold values from -4 to 4
- grad_table: bfloat16 [65536, 512], P(('dp', 'mp')), may hold values from -6 to 6
- weight_one: bfloat16 [128, 512], replicated, may hold values from -0.5 to 0.5
- weight_two: bfloat16 [512, 512], replicated, may hold values from -0.25 to 0.25
- grad_out: bfloat16 [65536, 512], P(('dp', 'mp')), may hold values from -6 to 6
Outputs:
- out_embed: bfloat16 [65536, 512], P(('dp', 'mp'))
- halo_grad: bfloat16 [65536, 512], P(('dp', 'mp'))
- grad_one: float32 [128, 512], replicated
- grad_two: float32 [512, 512], replicated
The draws below stay inside these ranges and needn't reach their ends.
Inputs may be any that keep to these rules, and one draw needn't show every extreme that they name: `halo_rows`: slot s of each device's 512 halo slots names a row of the block of 2048 rows held by device s // 16 of dp+mp (device index dp * 8 + mp), so that every device asks every owner for exactly 16 rows; rows may repeat.
All inputs are finite; a program needn't handle non-finite values.
Results may differ from the reference program's by a relative error of at most 0.006.
Values may be sent and summed in bfloat16 or wider, within the bound.
A program may use at most 128 MiB of HBM per device.

```python
import jax
import jax.numpy as jnp
from jax import lax

FEAT = 128
HID = 512
NB_DEV = 2048
HALO_DEV = 512
SHARD_ROWS = 2048
KB = 8
KH = 8
CAP = 16
BATCH = 65536
HALO_TOTAL = 16384
NODES = 65536
DEVICES = 32


def draw_halo_rows(key, part):
    slot_index = jnp.arange(HALO_TOTAL, dtype=jnp.int32)
    owner_index = slot_index % HALO_DEV // CAP
    offset_draw = jax.random.randint(key, (HALO_TOTAL,), 0, SHARD_ROWS, dtype=jnp.int32)
    row_ids = owner_index * SHARD_ROWS + offset_draw
    row_ids = row_ids.at[0].set(0)
    return row_ids.at[HALO_TOTAL - 1].set(NODES - 1)


def plant(entries, stream_key, least, top_value):
    place = [jax.random.randint(jax.random.fold_in(stream_key, axis), (), 0, length) for axis, length in enumerate(entries.shape)]
    widest = entries.shape.index(max(entries.shape))
    beside = place[:widest] + [(place[widest] + 1) % entries.shape[widest]] + place[widest + 1:]
    return entries.at[tuple(place)].set(least).at[tuple(beside)].set(top_value)


def block_levels(stream_key, shape, split, smallest, top_value):
    gain, own = 1.0, jax.random.fold_in(stream_key, 6)
    for axis_at, shards_of in split:
        draws = jnp.exp(jax.random.uniform(jax.random.fold_in(own, axis_at), (shards_of,), jnp.float32, smallest / len(split), top_value / len(split)))
        gain = gain * jnp.repeat(draws, shape[axis_at] // shards_of).reshape([-1 if axis == axis_at else 1 for axis in range(len(shape))])
    return gain


def bell_draw(key, dims, width, reach, split=(), kind=jnp.bfloat16):
    gain = block_levels(key, dims, split, -0.22, 0.18) if split else 1.0
    array = jax.random.normal(key, dims, jnp.float32) * width * gain
    return jnp.minimum(jnp.maximum(array, -reach), reach).astype(kind)


def setup_inputs(seed: int = 0) -> dict:
    splits = jax.random.split(jax.random.key(seed), 14)
    return {
        "node_feats": bell_draw(splits[0], (BATCH, FEAT), 1.0, 6.0, ((0, 32),)),
        "batch_deg": plant(jax.random.randint(splits[1], (BATCH,), 1, 9), jax.random.fold_in(splits[1], 1), 1, 8).astype(jnp.int32),
        "batch_nbrs": plant(jax.random.randint(splits[2], (BATCH, KB), 0, NB_DEV), jax.random.fold_in(splits[2], 1), 0, NB_DEV - 1).astype(jnp.int32),
        "halo_nbrs": plant(jax.random.randint(splits[3], (BATCH, KH), 0, HALO_DEV), jax.random.fold_in(splits[3], 1), 0, HALO_DEV - 1).astype(jnp.int32),
        "halo_len": plant(jax.random.randint(splits[4], (BATCH,), 1, KH + 1), jax.random.fold_in(splits[4], 1), 1, KH).astype(jnp.int32),
        "halo_rows": draw_halo_rows(jax.random.fold_in(splits[13], 71), 0),
        "halo_deg": plant(jax.random.randint(splits[6], (HALO_TOTAL,), 1, 9), jax.random.fold_in(splits[6], 1), 1, 8).astype(jnp.int32),
        "feat_table": bell_draw(splits[7], (NODES, FEAT), 1.0, 6.0, ((0, 32),)),
        "emb_table": bell_draw(splits[8], (NODES, HID), 0.5, 4.0, ((0, 32),)),
        "grad_table": bell_draw(splits[9], (NODES, HID), 1.0, 6.0, ((0, 32),)),
        "weight_one": bell_draw(splits[10], (FEAT, HID), FEAT ** -0.5, 0.5),
        "weight_two": bell_draw(splits[11], (HID, HID), HID ** -0.5, 0.25),
        "grad_out": bell_draw(splits[12], (BATCH, HID), 1.0, 6.0, ((0, 32),)),
    }


def matrices(batch_deg, batch_nbrs, halo_nbrs, halo_len, halo_deg):
    rows = batch_nbrs.shape[0]
    inv_batch = lax.rsqrt(batch_deg.astype(jnp.float32))
    inv_halo = lax.rsqrt(halo_deg.astype(jnp.float32))
    self_coef = 1.0 / batch_deg.astype(jnp.float32)
    nbr_coef = inv_batch[:, None] * inv_batch[batch_nbrs]
    valid = jnp.arange(halo_nbrs.shape[1], dtype=jnp.int32)[None, :] < halo_len[:, None]
    halo_coef = jnp.where(valid, inv_batch[:, None] * inv_halo[halo_nbrs], jnp.float32(0.0))
    row_index = jnp.arange(rows, dtype=jnp.int32)
    nbr_rows = jnp.broadcast_to(row_index[:, None], batch_nbrs.shape)
    halo_ids = jnp.broadcast_to(row_index[:, None], halo_nbrs.shape)
    adjacency = jnp.zeros((rows, rows), jnp.float32).at[nbr_rows, batch_nbrs].add(nbr_coef)
    adjacency = adjacency.at[row_index, row_index].add(self_coef).astype(jnp.bfloat16)
    halo_mat = jnp.zeros((rows, halo_deg.shape[0]), jnp.float32).at[halo_ids, halo_nbrs].add(halo_coef).astype(jnp.bfloat16)
    return (adjacency, halo_mat)

def mult(left, right):
    return jnp.dot(left.astype(jnp.float32), right.astype(jnp.float32))

def mult_t(left, right):
    return lax.dot_general(left.astype(jnp.float32), right.astype(jnp.float32), (((0,), (0,)), ((), ())))

def device_block(weight_one, weight_two, feats, degrees, nbr_idx, halo_idx, lengths, halo_degrees, halo_x, halo_e, halo_v, upstream):
    adjacency, halo_mat = matrices(degrees, nbr_idx, halo_idx, lengths, halo_degrees)
    agg_one = (mult(adjacency, feats) + mult(halo_mat, halo_x)).astype(jnp.bfloat16)
    pre_one = mult(agg_one, weight_one)
    hidden = jax.nn.silu(pre_one).astype(jnp.bfloat16)
    agg_two = (mult(adjacency, hidden) + mult(halo_mat, halo_e)).astype(jnp.bfloat16)
    out_block = mult(agg_two, weight_two).astype(jnp.bfloat16)
    spread = (mult_t(adjacency, upstream) + mult(halo_mat, halo_v)).astype(jnp.bfloat16)
    back_hidden = mult(spread, weight_two.T)
    sigma = jax.nn.sigmoid(pre_one)
    d_pre = (back_hidden * (sigma * (1.0 + pre_one * (1.0 - sigma)))).astype(jnp.bfloat16)
    term_two = mult_t(agg_two, upstream)
    term_one = mult_t(agg_one, d_pre)
    partial_value = mult_t(halo_mat, upstream)
    return (out_block, term_one, term_two, partial_value)

def reference(node_feats, batch_deg, batch_nbrs, halo_nbrs, halo_len, halo_rows, halo_deg, feat_table, emb_table, grad_table, weight_one, weight_two, grad_out):
    blocks = (node_feats.reshape(DEVICES, NB_DEV, FEAT), batch_deg.reshape(DEVICES, NB_DEV), batch_nbrs.reshape(DEVICES, NB_DEV, KB), halo_nbrs.reshape(DEVICES, NB_DEV, KH), halo_len.reshape(DEVICES, NB_DEV), halo_rows.reshape(DEVICES, HALO_DEV), halo_deg.reshape(DEVICES, HALO_DEV), grad_out.reshape(DEVICES, NB_DEV, HID))

    def step_fn(carry, inputs):
        feats, degrees, nbr_idx, halo_idx, lengths, slot_rows, halo_degrees, upstream = inputs
        out_block, term_one, term_two, partial_value = device_block(weight_one, weight_two, feats, degrees, nbr_idx, halo_idx, lengths, halo_degrees, feat_table[slot_rows], emb_table[slot_rows], grad_table[slot_rows], upstream)
        return ((carry[0] + term_one, carry[1] + term_two), (out_block, partial_value))
    start = (jnp.zeros((FEAT, HID), jnp.float32), jnp.zeros((HID, HID), jnp.float32))
    sums, outputs = lax.scan(step_fn, start, blocks)
    out_embed = outputs[0].reshape(BATCH, HID)
    partials = outputs[1].reshape(HALO_TOTAL, HID)
    halo_grad = jnp.zeros((NODES, HID), jnp.float32).at[halo_rows].add(partials).astype(jnp.bfloat16)
    factor = 1.0 / jnp.sqrt(jnp.float32(BATCH))
    return (out_embed, halo_grad, sums[0] * factor, sums[1] * factor)
```

```python
import functools

import jax
import jax.numpy as jnp
from jax import lax
from jax.experimental import pallas as pl
from jax.experimental.pallas import tpu as pltpu
from jax.sharding import PartitionSpec as P

F32 = jnp.float32
BF16 = jnp.bfloat16
I32 = jnp.int32
LANES = 128
CHUNK = 256
NN = (((1,), (0,)), ((), ()))
NT = (((1,), (1,)), ((), ()))
TN = (((0,), (0,)), ((), ()))


def dot(left, right, dims=NN):
    return lax.dot_general(left, right, dims, preferred_element_type=F32)


def kernel(
    size_dp,
    size_mp,
    per_peer,
    factor,
    packed_hbm,
    feats_hbm,
    feat_hbm,
    emb_hbm,
    gradt_hbm,
    w1_hbm,
    w2_hbm,
    up_hbm,
    out_hbm,
    hgrad_hbm,
    g1_ref,
    g2_ref,
    packed,
    feats,
    feat_tab,
    emb_tab,
    grad_tab,
    w1,
    w2,
    up,
    ask_src,
    ask_mid,
    ask_turn,
    ask_fin,
    inv_col,
    hinv_col,
    adj_t,
    hal_t,
    sel,
    x_src,
    x_mid,
    x_fin,
    e_src,
    e_mid,
    e_fin,
    v_src,
    v_mid,
    v_fin,
    p_src,
    p_mid,
    p_fin,
    feats_t,
    agg1_t,
    hid_t,
    dfac_t,
    own2_t,
    agg2_t,
    spread_own,
    term1,
    term2,
    out_buf,
    hgrad_buf,
    t1_src,
    t1_mid,
    t1_sum,
    t1_fin,
    t1_all,
    t2_src,
    t2_mid,
    t2_sum,
    t2_fin,
    t2_all,
    load_sem,
    store_sem,
    self_sem,
    send_mp,
    recv_mp,
    send_dp,
    recv_dp,
):
    me_dp = lax.axis_index("dp")
    me_mp = lax.axis_index("mp")
    rows = adj_t.shape[0]
    halo = hal_t.shape[0]
    group = size_mp * per_peer

    def load(at, source, target):
        return pltpu.make_async_copy(source, target, load_sem.at[at])

    loads = {
        "packed": load(0, packed_hbm, packed),
        "emb": load(1, emb_hbm, emb_tab),
        "feat": load(2, feat_hbm, feat_tab),
        "gradt": load(3, gradt_hbm, grad_tab),
        "up": load(4, up_hbm, up),
        "feats": load(5, feats_hbm, feats),
        "w1": load(6, w1_hbm, w1),
        "w2": load(7, w2_hbm, w2),
    }
    for name in ("packed", "feat", "emb", "gradt", "up", "feats", "w1", "w2"):
        loads[name].start()

    peers_mp = [lax.rem(me_mp + step, size_mp) for step in range(1, size_mp)]
    peers_dp = [lax.rem(me_dp + step, size_dp) for step in range(1, size_dp)]
    barrier = pltpu.get_barrier_semaphore()
    for peer in peers_mp:
        pl.semaphore_signal(barrier, inc=1, device_id=(me_dp, peer), device_id_type=pl.DeviceIdType.MESH)
    for peer in peers_dp:
        pl.semaphore_signal(barrier, inc=1, device_id=(peer, me_mp), device_id_type=pl.DeviceIdType.MESH)
    pl.semaphore_wait(barrier, size_mp - 1 + size_dp - 1)

    def to_mp(piece, peer, place, source, target):
        return pltpu.make_async_remote_copy(
            src_ref=source,
            dst_ref=target,
            send_sem=send_mp.at[piece, peer],
            recv_sem=recv_mp.at[piece, place],
            device_id=(me_dp, peer),
            device_id_type=pl.DeviceIdType.MESH,
        )

    def to_dp(piece, peer, place, source, target):
        return pltpu.make_async_remote_copy(
            src_ref=source,
            dst_ref=target,
            send_sem=send_dp.at[piece, peer],
            recv_sem=recv_dp.at[piece, place],
            device_id=(peer, me_mp),
            device_id_type=pl.DeviceIdType.MESH,
        )

    class Hop:
        def __init__(self, make, piece, me, peers, source_at, target_at, at):
            self.own = lambda: pltpu.make_async_copy(source_at(me), target_at(me), self_sem.at[at])
            self.out = [make(piece, peer, me, source_at(peer), target_at(me)) for peer in peers]
            self.come = [make(piece, peer, peer, source_at(peer), target_at(peer)) for peer in peers]

        def start(self):
            for copy in self.out:
                copy.start()
            self.own().start()

        def arrive(self):
            self.own().wait()
            for copy in self.come:
                copy.wait_recv()

        def finish(self):
            for copy in self.out:
                copy.wait_send()

    def block(ref, peer):
        return ref.at[:, pl.ds(pl.multiple_of(peer * per_peer, per_peer), per_peer), :]

    hops = []

    def hop_mp(piece, source_at, target_at):
        hop = Hop(to_mp, piece, me_mp, peers_mp, source_at, target_at, len(hops))
        hops.append(hop)
        return hop

    def hop_dp(piece, source_at, target_at):
        hop = Hop(to_dp, piece, me_dp, peers_dp, source_at, target_at, len(hops))
        hops.append(hop)
        return hop

    def swap(piece, source, middle, final):
        first = hop_mp(piece, lambda peer: block(source, peer), lambda peer: block(middle, peer))
        second = hop_dp(piece, lambda peer: middle.at[peer], lambda peer: final.at[peer])
        return first, second

    ask_one = hop_mp(0, lambda peer: ask_src, lambda peer: ask_mid.at[peer])
    ask_two = hop_dp(0, lambda peer: ask_turn.at[peer], lambda peer: ask_fin.at[peer])
    x_one, x_two = swap(1, x_src, x_mid, x_fin)
    e_one, e_two = swap(2, e_src, e_mid, e_fin)
    v_one, v_two = swap(3, v_src, v_mid, v_fin)
    p_one, p_two = swap(4, p_src, p_mid, p_fin)
    t2_one = hop_mp(5, lambda peer: t2_src.at[peer], lambda peer: t2_mid.at[peer])
    t2_two = hop_dp(5, lambda peer: t2_sum, lambda peer: t2_fin.at[peer])
    t1_one = hop_mp(6, lambda peer: t1_src.at[peer], lambda peer: t1_mid.at[peer])
    t1_two = hop_dp(6, lambda peer: t1_sum, lambda peer: t1_fin.at[peer])
    t2_three = hop_mp(7, lambda peer: t2_all.at[me_mp], lambda peer: t2_all.at[peer])
    t1_three = hop_mp(8, lambda peer: t1_all.at[me_mp], lambda peer: t1_all.at[peer])

    def gather_start(hop):
        for copy in hop.out:
            copy.start()

    def gather_arrive(hop):
        for copy in hop.come:
            copy.wait_recv()

    loads["packed"].wait()
    slots = batch_slots = 8
    line = 2 * batch_slots
    for part in range(size_dp):
        offsets = packed[line + 2 : line + 3, halo + part * group : halo + (part + 1) * group]
        ask_src[part * 8 : part * 8 + 8, :] = jnp.broadcast_to(offsets, (8, group))
    ask_one.start()

    inv_row = lax.rsqrt(packed[line : line + 1, :].astype(F32))
    hinv_row = lax.rsqrt(packed[line + 2 : line + 3, 0:halo].astype(F32))
    for at in range(rows // LANES):
        piece = inv_row[:, at * LANES : (at + 1) * LANES]
        inv_col[at * LANES : (at + 1) * LANES, :] = jnp.broadcast_to(piece, (LANES, LANES)).T
    for at in range(halo // LANES):
        piece = hinv_row[:, at * LANES : (at + 1) * LANES]
        hinv_col[at * LANES : (at + 1) * LANES, :] = jnp.broadcast_to(piece, (LANES, LANES)).T

    def fill(target, column, words_rows, first, extra, scale_col, lanes):
        row_at = lax.broadcasted_iota(I32, (words_rows, LANES), 0)
        words = jnp.zeros((words_rows, LANES), I32)
        shift_by = words_rows.bit_length() - 1
        picks = []
        for slot in range(slots):
            index = packed[first + slot : first + slot + 1, lanes]
            value = lax.shift_left(jnp.ones_like(index), 4 * lax.shift_right_logical(index, shift_by))
            if extra is None:
                length = packed[line + 1 : line + 2, lanes]
                value = jnp.where(length > slot, value, 0)
            picks.append((index, value))
        if extra is not None:
            value = lax.shift_left(jnp.ones_like(extra), 4 * lax.shift_right_logical(extra, shift_by))
            picks.append((extra, value))
        for index, value in picks:
            low = jnp.bitwise_and(index, words_rows - 1)
            words = words + jnp.where(low == row_at, value, 0)
        inv_here = lax.rsqrt(packed[line : line + 1, lanes].astype(F32))
        for nibble in range(8):
            count = jnp.bitwise_and(lax.shift_right_logical(words, 4 * nibble), 15)
            span = slice(nibble * words_rows, (nibble + 1) * words_rows)
            tile = count.astype(F32) * (scale_col[span, :] * inv_here)
            target[span, lanes] = tile.astype(BF16)

    def fill_halo(column, carry):
        lanes = pl.ds(pl.multiple_of(column * LANES, LANES), LANES)
        fill(hal_t, column, halo // 8, batch_slots, None, hinv_col, lanes)
        return carry

    def fill_adj(column, carry):
        lanes = pl.ds(pl.multiple_of(column * LANES, LANES), LANES)
        own = lax.broadcasted_iota(I32, (1, LANES), 1) + column * LANES
        fill(adj_t, column, rows // 8, 0, own, inv_col, lanes)
        return carry

    columns = rows // LANES
    lax.fori_loop(0, columns, fill_halo, 0)

    ask_one.arrive()
    lane_group = lax.broadcasted_iota(I32, (size_dp * 8, group), 1) // per_peer
    turned = jnp.zeros((size_dp * 8, group), I32)
    for source in range(size_mp):
        shift = lax.rem(source - me_mp + size_mp, size_mp) * per_peer
        moved = pltpu.roll(ask_mid[source], shift, 1)
        turned = jnp.where(lane_group == source, moved, turned)
    for part in range(size_dp):
        ask_turn[part] = turned[part * 8 : part * 8 + 8, :]
    ask_two.start()

    lax.fori_loop(0, columns // 4, fill_adj, 0)

    ask_two.arrive()
    lane_at = lax.broadcasted_iota(I32, (group, LANES), 1)
    for part in range(size_dp):
        ask_col = jnp.broadcast_to(ask_fin[part, 0:1, :], (LANES, group)).T

        def fill_sel(column, carry, ask_col=ask_col, part=part):
            lanes = pl.ds(pl.multiple_of(column * LANES, LANES), LANES)
            hit = ask_col == lane_at + column * LANES
            sel[part * group : (part + 1) * group, lanes] = jnp.where(hit, 1.0, 0.0).astype(BF16)
            return carry

        lax.fori_loop(0, columns, fill_sel, 0)

    def pick(table, target):
        def body(part, carry):
            here = pl.ds(pl.multiple_of(part * group, group), group)
            target[part] = dot(sel[here, :], table[...]).astype(BF16)
            return carry

        lax.fori_loop(0, size_dp, body, 0)

    loads["feat"].wait()
    pick(feat_tab, x_src)
    x_one.start()
    loads["emb"].wait()
    pick(emb_tab, e_src)
    e_one.start()
    loads["gradt"].wait()
    pick(grad_tab, v_src)
    v_one.start()

    lax.fori_loop(columns // 4, columns, fill_adj, 0)

    x_one.arrive()
    x_two.start()

    chunks = rows // CHUNK

    def at_chunk(step):
        return pl.ds(pl.multiple_of(step * CHUNK, CHUNK), CHUNK)

    loads["up"].wait()
    for part in range(size_dp):
        p_src[part] = dot(hal_t[part * group : (part + 1) * group, :], up[...]).astype(BF16)

    e_one.arrive()
    e_two.start()

    def own_spread(step, carry):
        here = at_chunk(step)
        spread_own[here, :] = dot(adj_t[here, :], up[...])
        return carry

    lax.fori_loop(0, chunks // 2, own_spread, 0)
    v_one.arrive()
    v_two.start()
    p_one.start()
    lax.fori_loop(chunks // 2, chunks, own_spread, 0)

    loads["feats"].wait()
    feats_t[...] = feats[...].T
    loads["w1"].wait()
    w1_t = w1[...].T
    x_two.arrive()
    hx_t = x_fin[...].reshape(halo, x_fin.shape[-1]).T

    def layer_one(step, carry):
        here = at_chunk(step)
        agg = (dot(feats_t[...], adj_t[:, here]) + dot(hx_t, hal_t[:, here])).astype(BF16)
        agg1_t[:, here] = agg
        pre = dot(w1_t, agg)
        sigma = jax.nn.sigmoid(pre)
        hid_t[:, here] = (pre * sigma).astype(BF16)
        dfac_t[:, here] = sigma * (1.0 + pre * (1.0 - sigma))
        return carry

    lax.fori_loop(0, chunks, layer_one, 0)

    def own_two(step, carry):
        here = at_chunk(step)
        own2_t[:, here] = dot(hid_t[...], adj_t[:, here])
        return carry

    lax.fori_loop(0, chunks, own_two, 0)

    p_one.arrive()
    p_two.start()

    e_two.arrive()
    he_t = e_fin[...].reshape(halo, e_fin.shape[-1]).T

    def layer_two(step, carry):
        here = at_chunk(step)
        agg2_t[:, here] = (own2_t[:, here] + dot(he_t, hal_t[:, here])).astype(BF16)
        return carry

    lax.fori_loop(0, chunks, layer_two, 0)
    part2 = t2_src.shape[1]
    for peer in range(size_mp):
        strip = agg2_t[peer * part2 : (peer + 1) * part2, :]
        t2_src[peer] = dot(strip, up[...]).astype(BF16)
    t2_one.start()

    loads["w2"].wait()
    v_two.arrive()
    term1[...] = jnp.zeros_like(term1)
    hv = v_fin[...].reshape(halo, v_fin.shape[-1])

    def backward(step, carry):
        here = at_chunk(step)
        spread = (spread_own[here, :] + dot(hal_t[:, here], hv, TN)).astype(BF16)
        back = dot(w2[...], spread, NT)
        d_pre = (back * dfac_t[:, here]).astype(BF16)
        term1[...] += dot(agg1_t[:, here], d_pre, NT)
        return carry

    lax.fori_loop(0, chunks, backward, 0)
    part1 = t1_src.shape[1]
    for peer in range(size_mp):
        t1_src[peer] = term1[peer * part1 : (peer + 1) * part1, :].astype(BF16)
    t1_one.start()

    def total(ref, count):
        value = ref[0].astype(F32)
        for at in range(1, count):
            value = value + ref[at].astype(F32)
        return value

    t2_one.arrive()
    t2_sum[...] = total(t2_mid, size_mp).astype(BF16)
    t2_two.start()

    def output(step, carry):
        here = at_chunk(step)
        out_buf[here, :] = dot(agg2_t[:, here], w2[...], TN).astype(BF16)
        return carry

    lax.fori_loop(0, chunks, output, 0)
    out_store = pltpu.make_async_copy(out_buf, out_hbm, store_sem.at[0])
    out_store.start()

    t1_one.arrive()
    t1_sum[...] = total(t1_mid, size_mp).astype(BF16)
    t1_two.start()
    t2_two.arrive()
    t2_all[me_mp] = (total(t2_fin, size_dp) * factor).astype(BF16)
    gather_start(t2_three)

    p_two.arrive()
    hp = p_fin[...].reshape(halo, p_fin.shape[-1])

    def owner_sum(step, carry):
        here = at_chunk(step)
        hgrad_buf[here, :] = dot(sel[:, here], hp, TN).astype(BF16)
        return carry

    lax.fori_loop(0, chunks // 2, owner_sum, 0)
    t1_two.arrive()
    t1_all[me_mp] = (total(t1_fin, size_dp) * factor).astype(BF16)
    gather_start(t1_three)
    lax.fori_loop(chunks // 2, chunks, owner_sum, 0)
    hgrad_store = pltpu.make_async_copy(hgrad_buf, hgrad_hbm, store_sem.at[1])
    hgrad_store.start()

    gather_arrive(t2_three)
    for peer in range(size_mp):
        g2_ref[peer * part2 : (peer + 1) * part2, :] = t2_all[peer].astype(F32)
    gather_arrive(t1_three)
    for peer in range(size_mp):
        g1_ref[peer * part1 : (peer + 1) * part1, :] = t1_all[peer].astype(F32)
    for hop in hops:
        hop.finish()
    out_store.wait()
    hgrad_store.wait()


def local_kernel(
    node_feats,
    batch_deg,
    batch_nbrs,
    halo_nbrs,
    halo_len,
    halo_rows,
    halo_deg,
    feat_table,
    emb_table,
    grad_table,
    weight_one,
    weight_two,
    grad_out,
):
    size_dp = lax.axis_size("dp")
    size_mp = lax.axis_size("mp")
    rows, feat = node_feats.shape
    halo = halo_rows.shape[0]
    shard_rows = feat_table.shape[0]
    hid_in, hid = weight_two.shape
    per_peer = halo // (size_dp * size_mp)
    group = size_mp * per_peer
    factor = 1.0 / float(rows * size_dp * size_mp) ** 0.5
    tail = jnp.concatenate([halo_deg, halo_rows % shard_rows, jnp.zeros((rows - 2 * halo,), I32)])
    packed = jnp.concatenate(
        [
            batch_nbrs.T,
            halo_nbrs.T,
            batch_deg[None],
            halo_len[None],
            tail[None],
            jnp.zeros((5, rows), I32),
        ]
    )
    any_spec = pl.BlockSpec(memory_space=pl.ANY)
    vmem_spec = pl.BlockSpec(memory_space=pltpu.VMEM)
    vmem = pltpu.VMEM
    part1, part2 = feat // size_mp, hid // size_mp

    def three(width):
        return [vmem((size_dp, group, width), BF16)] * 3

    def sums(part):
        return [
            vmem((size_mp, part, hid), BF16),
            vmem((size_mp, part, hid), BF16),
            vmem((part, hid), BF16),
            vmem((size_dp, part, hid), BF16),
            vmem((size_mp, part, hid), BF16),
        ]

    return pl.pallas_call(
        functools.partial(kernel, size_dp, size_mp, per_peer, factor),
        out_shape=(
            jax.ShapeDtypeStruct((rows, hid), BF16),
            jax.ShapeDtypeStruct((shard_rows, hid), BF16),
            jax.ShapeDtypeStruct((feat, hid), F32),
            jax.ShapeDtypeStruct((hid_in, hid), F32),
        ),
        in_specs=[any_spec] * 8,
        out_specs=(any_spec, any_spec, vmem_spec, vmem_spec),
        scratch_shapes=[
            vmem(packed.shape, I32),
            vmem(node_feats.shape, BF16),
            vmem(feat_table.shape, BF16),
            vmem(emb_table.shape, BF16),
            vmem(grad_table.shape, BF16),
            vmem(weight_one.shape, BF16),
            vmem(weight_two.shape, BF16),
            vmem(grad_out.shape, BF16),
            vmem((size_dp * 8, group), I32),
            vmem((size_mp, size_dp * 8, group), I32),
            vmem((size_dp, 8, group), I32),
            vmem((size_dp, 8, group), I32),
            vmem((rows, LANES), F32),
            vmem((halo, LANES), F32),
            vmem((rows, rows), BF16),
            vmem((halo, rows), BF16),
            vmem((halo, shard_rows), BF16),
            *three(feat),
            *three(hid),
            *three(hid),
            *three(hid),
            vmem((feat, rows), BF16),
            vmem((feat, rows), BF16),
            vmem((hid, rows), BF16),
            vmem((hid, rows), F32),
            vmem((hid, rows), F32),
            vmem((hid, rows), BF16),
            vmem((rows, hid), F32),
            vmem((feat, hid), F32),
            vmem((8, LANES), F32),
            vmem((rows, hid), BF16),
            vmem((shard_rows, hid), BF16),
            *sums(part1),
            *sums(part2),
            pltpu.SemaphoreType.DMA((8,)),
            pltpu.SemaphoreType.DMA((2,)),
            pltpu.SemaphoreType.DMA((16,)),
            pltpu.SemaphoreType.DMA((9, size_mp)),
            pltpu.SemaphoreType.DMA((9, size_mp)),
            pltpu.SemaphoreType.DMA((7, size_dp)),
            pltpu.SemaphoreType.DMA((7, size_dp)),
        ],
        compiler_params=pltpu.CompilerParams(
            collective_id=0, has_side_effects=True, vmem_limit_bytes=60 * 1024 * 1024
        ),
    )(packed, node_feats, feat_table, emb_table, grad_table, weight_one, weight_two, grad_out)


def matrices(batch_deg, batch_nbrs, halo_nbrs, halo_len, halo_deg):
    rows = batch_nbrs.shape[0]
    halo_count = halo_deg.shape[0]
    inv_batch = lax.rsqrt(batch_deg.astype(jnp.float32))
    inv_halo = lax.rsqrt(halo_deg.astype(jnp.float32))
    self_coef = 1.0 / batch_deg.astype(jnp.float32)
    row_index = jnp.arange(rows, dtype=jnp.int32)
    halo_index = jnp.arange(halo_count, dtype=jnp.int32)
    counts = jnp.zeros((rows, rows), jnp.float32)
    for slot in range(batch_nbrs.shape[1]):
        counts = counts + (batch_nbrs[:, slot, None] == row_index[None, :]).astype(jnp.float32)
    halo_counts = jnp.zeros((rows, halo_count), jnp.float32)
    for slot in range(halo_nbrs.shape[1]):
        hit = (halo_nbrs[:, slot, None] == halo_index[None, :]) & (halo_len[:, None] > slot)
        halo_counts = halo_counts + hit.astype(jnp.float32)
    diagonal = jnp.where(
        row_index[:, None] == row_index[None, :], self_coef[:, None], jnp.float32(0.0)
    )
    adjacency = (counts * (inv_batch[:, None] * inv_batch[None, :]) + diagonal).astype(jnp.bfloat16)
    halo_mat = (halo_counts * (inv_batch[:, None] * inv_halo[None, :])).astype(jnp.bfloat16)
    return (adjacency, halo_mat)


def mult(left, right):
    return jnp.dot(left, right, preferred_element_type=jnp.float32)


def mult_t(left, right):
    return lax.dot_general(
        left, right, (((0,), (0,)), ((), ())), preferred_element_type=jnp.float32
    )


def local_plain(
    node_feats,
    batch_deg,
    batch_nbrs,
    halo_nbrs,
    halo_len,
    halo_rows,
    halo_deg,
    feat_table,
    emb_table,
    grad_table,
    weight_one,
    weight_two,
    grad_out,
):
    batch_rows = node_feats.shape[0]
    hidden_width = weight_two.shape[1]
    feat_width = feat_table.shape[1]
    size_dp = lax.axis_size("dp")
    size_mp = lax.axis_size("mp")
    devices = size_dp * size_mp
    halo_count = halo_rows.shape[0]
    per_peer = halo_count // devices
    shard_rows = feat_table.shape[0]
    offsets = halo_rows % shard_rows
    asked = lax.all_to_all(
        offsets.reshape(devices, per_peer), ("dp", "mp"), split_axis=0, concat_axis=0, tiled=True
    )
    shard_index = jnp.arange(shard_rows, dtype=jnp.int32)
    selector = (asked.reshape(-1)[:, None] == shard_index[None, :]).astype(jnp.bfloat16)
    lead = asked.shape
    picked_x = mult(selector, feat_table).astype(jnp.bfloat16).reshape(lead + (feat_width,))
    picked_e = mult(selector, emb_table).astype(jnp.bfloat16).reshape(lead + (hidden_width,))
    picked_v = mult(selector, grad_table).astype(jnp.bfloat16).reshape(lead + (hidden_width,))
    pulled = (
        lax.all_to_all(picked_x, ("dp", "mp"), split_axis=0, concat_axis=0, tiled=True),
        lax.all_to_all(picked_e, ("dp", "mp"), split_axis=0, concat_axis=0, tiled=True),
        lax.all_to_all(picked_v, ("dp", "mp"), split_axis=0, concat_axis=0, tiled=True),
    )
    halo_x = pulled[0].reshape(halo_count, feat_width)
    halo_e = pulled[1].reshape(halo_count, hidden_width)
    halo_v = pulled[2].reshape(halo_count, hidden_width)
    adjacency, halo_mat = matrices(batch_deg, batch_nbrs, halo_nbrs, halo_len, halo_deg)
    agg_one = (mult(adjacency, node_feats) + mult(halo_mat, halo_x)).astype(jnp.bfloat16)
    pre_one = mult(agg_one, weight_one)
    hidden = jax.nn.silu(pre_one).astype(jnp.bfloat16)
    agg_two = (mult(adjacency, hidden) + mult(halo_mat, halo_e)).astype(jnp.bfloat16)
    out_embed = mult(agg_two, weight_two).astype(jnp.bfloat16)
    partial_value = mult_t(halo_mat, grad_out)
    arrived = lax.all_to_all(
        partial_value.reshape(devices, per_peer, hidden_width),
        ("dp", "mp"),
        split_axis=0,
        concat_axis=0,
        tiled=True,
    )
    halo_grad = lax.dot_general(
        selector.astype(jnp.float32),
        arrived.reshape(-1, hidden_width),
        (((0,), (0,)), ((), ())),
        precision=lax.Precision.HIGHEST,
        preferred_element_type=jnp.float32,
    )
    halo_grad = halo_grad.astype(jnp.bfloat16)
    spread = (mult_t(adjacency, grad_out) + mult(halo_mat, halo_v)).astype(jnp.bfloat16)
    back_hidden = lax.dot_general(
        spread, weight_two, (((1,), (1,)), ((), ())), preferred_element_type=jnp.float32
    )
    sigma = jax.nn.sigmoid(pre_one)
    d_pre = (back_hidden * (sigma * (1.0 + pre_one * (1.0 - sigma)))).astype(jnp.bfloat16)
    term_two = mult_t(agg_two, grad_out)
    term_one = mult_t(agg_one, d_pre)
    column_sums = (
        lax.psum_scatter(term_one, "mp", scatter_dimension=1, tiled=True),
        lax.psum_scatter(term_two, "mp", scatter_dimension=1, tiled=True),
    )
    column_sums = lax.psum((column_sums[0], column_sums[1]), "dp")
    summed = (
        lax.all_gather(column_sums[0], "mp", axis=1, tiled=True),
        lax.all_gather(column_sums[1], "mp", axis=1, tiled=True),
    )
    factor = 1.0 / jnp.sqrt(jnp.float32(batch_rows * devices))
    return (out_embed, halo_grad, summed[0] * factor, summed[1] * factor)


def local(*args):
    size_dp, size_mp = lax.axis_size("dp"), lax.axis_size("mp")
    rows, halo = args[0].shape[0], args[5].shape[0]
    per_peer = halo // (size_dp * size_mp)
    if per_peer % 16 == 0 and size_mp * per_peer == LANES and rows == args[7].shape[0]:
        return local_kernel(*args)
    return local_plain(*args)


def solution(mesh):
    return jax.shard_map(
        local,
        mesh=mesh,
        in_specs=(
            P(("dp", "mp"), None),
            P(("dp", "mp")),
            P(("dp", "mp"), None),
            P(("dp", "mp"), None),
            P(("dp", "mp")),
            P(("dp", "mp")),
            P(("dp", "mp")),
            P(("dp", "mp"), None),
            P(("dp", "mp"), None),
            P(("dp", "mp"), None),
            P(),
            P(),
            P(("dp", "mp"), None),
        ),
        out_specs=(P(("dp", "mp"), None), P(("dp", "mp"), None), P(), P()),
        check_vma=False,
    )
```

```python
import functools

import jax
import jax.numpy as jnp
from jax import lax
from jax.experimental import pallas as pl
from jax.experimental.pallas import tpu as pltpu
from jax.sharding import PartitionSpec as P

F32 = jnp.float32
BF16 = jnp.bfloat16
I32 = jnp.int32
LANES = 128
CHUNK = 256
VMEM_MIB = 54
NN = (((1,), (0,)), ((), ()))
NT = (((1,), (1,)), ((), ()))
TN = (((0,), (0,)), ((), ()))


def dot(left, right, dims=NN):
    return lax.dot_general(left, right, dims, preferred_element_type=F32)


def kernel(
    size_dp,
    size_mp,
    per_peer,
    factor,
    nbrs_hbm,
    hnbrs_hbm,
    deg_hbm,
    len_hbm,
    hdeg_hbm,
    hrows_hbm,
    feats_hbm,
    feat_hbm,
    emb_hbm,
    gradt_hbm,
    w1_hbm,
    w2_hbm,
    up_hbm,
    out_buf,
    hgrad_buf,
    g1_ref,
    g2_ref,
    nbrs,
    hnbrs,
    deg,
    length,
    hdeg,
    hrows,
    feats,
    feat_tab,
    emb_tab,
    grad_tab,
    w1,
    w2,
    up,
    ask_src,
    ask_mid,
    ask_turn,
    ask_fin,
    ask_col_ref,
    inv_col,
    hinv_col,
    adj_t,
    hal_t,
    sel,
    x_src,
    x_mid,
    x_fin,
    e_src,
    e_mid,
    e_fin,
    v_src,
    v_mid,
    v_fin,
    p_src,
    p_mid,
    p_fin,
    q_src,
    q_mid,
    q_fin,
    feats_t,
    agg1_t,
    hid_t,
    dfac_t,
    own2_t,
    agg2_t,
    spread_own,
    term1,
    hal,
    t1_src,
    t1_mid,
    t1_sum,
    t1_fin,
    t1_all,
    t2_src,
    t2_mid,
    t2_sum,
    t2_fin,
    t2_all,
    load_sem,
    self_sem,
    send_mp,
    recv_mp,
    send_dp,
    recv_dp,
):
    me_dp = lax.axis_index("dp")
    me_mp = lax.axis_index("mp")
    rows = adj_t.shape[0]
    halo = hal_t.shape[0]
    group = size_mp * per_peer
    shard_rows = sel.shape[1]

    def load(at, source, target):
        return pltpu.make_async_copy(source, target, load_sem.at[at])

    loads = {
        "hrows": load(0, hrows_hbm, hrows),
        "nbrs": load(8, nbrs_hbm, nbrs),
        "hnbrs": load(9, hnbrs_hbm, hnbrs),
        "deg": load(10, deg_hbm, deg),
        "length": load(11, len_hbm, length),
        "hdeg": load(12, hdeg_hbm, hdeg),
        "emb": load(1, emb_hbm, emb_tab),
        "feat": load(2, feat_hbm, feat_tab),
        "gradt": load(3, gradt_hbm, grad_tab),
        "up": load(4, up_hbm, up),
        "feats": load(5, feats_hbm, feats),
        "w1": load(6, w1_hbm, w1),
        "w2": load(7, w2_hbm, w2),
    }
    for name in ("hrows", "deg", "hdeg", "length", "hnbrs", "nbrs", "up"):
        loads[name].start()
    for name in ("feat", "emb", "gradt", "feats", "w1", "w2"):
        loads[name].start()

    peers_mp = [lax.rem(me_mp + step, size_mp) for step in range(1, size_mp)]
    peers_dp = [lax.rem(me_dp + step, size_dp) for step in range(1, size_dp)]
    barrier = pltpu.get_barrier_semaphore()
    for peer in peers_mp:
        pl.semaphore_signal(barrier, inc=1, device_id=(me_dp, peer), device_id_type=pl.DeviceIdType.MESH)
    for peer in peers_dp:
        pl.semaphore_signal(barrier, inc=1, device_id=(peer, me_mp), device_id_type=pl.DeviceIdType.MESH)
    pl.semaphore_wait(barrier, size_mp - 1 + size_dp - 1)

    def to_mp(piece, peer, place, source, target):
        return pltpu.make_async_remote_copy(
            src_ref=source,
            dst_ref=target,
            send_sem=send_mp.at[piece, peer],
            recv_sem=recv_mp.at[piece, place],
            device_id=(me_dp, peer),
            device_id_type=pl.DeviceIdType.MESH,
        )

    def to_dp(piece, peer, place, source, target):
        return pltpu.make_async_remote_copy(
            src_ref=source,
            dst_ref=target,
            send_sem=send_dp.at[piece, peer],
            recv_sem=recv_dp.at[piece, place],
            device_id=(peer, me_mp),
            device_id_type=pl.DeviceIdType.MESH,
        )

    class Hop:
        def __init__(self, make, piece, me, peers, source_at, target_at, at):
            self.own = lambda: pltpu.make_async_copy(source_at(me), target_at(me), self_sem.at[at])
            self.out = [make(piece, peer, me, source_at(peer), target_at(me)) for peer in peers]
            self.come = [make(piece, peer, peer, source_at(peer), target_at(peer)) for peer in peers]

        def start(self):
            for copy in self.out:
                copy.start()
            self.own().start()

        def arrive(self):
            self.own().wait()
            for copy in self.come:
                copy.wait_recv()

        def finish(self):
            for copy in self.out:
                copy.wait_send()

    def block(ref, peer):
        return ref.at[:, pl.ds(pl.multiple_of(peer * per_peer, per_peer), per_peer), :]

    hops = []

    def hop_mp(piece, source_at, target_at):
        hop = Hop(to_mp, piece, me_mp, peers_mp, source_at, target_at, len(hops))
        hops.append(hop)
        return hop

    def hop_dp(piece, source_at, target_at):
        hop = Hop(to_dp, piece, me_dp, peers_dp, source_at, target_at, len(hops))
        hops.append(hop)
        return hop

    def swap(piece, source, middle, final):
        first = hop_mp(piece, lambda peer: block(source, peer), lambda peer: block(middle, peer))
        second = hop_dp(piece, lambda peer: middle.at[peer], lambda peer: final.at[peer])
        return first, second

    ask_one = hop_mp(0, lambda peer: ask_src, lambda peer: ask_mid.at[peer])
    ask_two = hop_dp(0, lambda peer: ask_turn.at[peer], lambda peer: ask_fin.at[peer])
    x_one, x_two = swap(1, x_src, x_mid, x_fin)
    e_one, e_two = swap(2, e_src, e_mid, e_fin)
    v_one, v_two = swap(3, v_src, v_mid, v_fin)
    p_one, p_two = swap(4, p_src, p_mid, p_fin)
    q_one, q_two = swap(7, q_src, q_mid, q_fin)
    t2_one = hop_mp(5, lambda peer: t2_src.at[peer], lambda peer: t2_mid.at[peer])
    t2_two = hop_dp(5, lambda peer: t2_sum, lambda peer: t2_fin.at[peer])
    t1_one = hop_mp(6, lambda peer: t1_src.at[peer], lambda peer: t1_mid.at[peer])
    t1_two = hop_dp(6, lambda peer: t1_sum, lambda peer: t1_fin.at[peer])
    t2_three = hop_mp(8, lambda peer: t2_all.at[me_mp], lambda peer: t2_all.at[peer])
    t1_three = hop_mp(9, lambda peer: t1_all.at[me_mp], lambda peer: t1_all.at[peer])

    def gather_start(hop):
        for copy in hop.out:
            copy.start()

    def gather_arrive(hop):
        for copy in hop.come:
            copy.wait_recv()

    loads["hrows"].wait()
    for part in range(size_dp):
        offsets = lax.rem(hrows[part : part + 1, :], shard_rows)
        ask_src[part * 8 : part * 8 + 8, :] = jnp.broadcast_to(offsets, (8, group))
    ask_one.start()

    for name in ("deg", "hdeg", "length", "hnbrs"):
        loads[name].wait()

    def spread_out(target, source):
        for at in range(source.shape[0]):
            piece = lax.rsqrt(source[at : at + 1, :].astype(F32))
            target[at * LANES : (at + 1) * LANES, :] = jnp.broadcast_to(piece, (LANES, LANES)).T

    spread_out(hinv_col, hdeg)

    def fill(target, column, words_rows, indices, extra, scale_col, lanes):
        row_at = lax.broadcasted_iota(I32, (words_rows, LANES), 0)
        words = jnp.zeros((words_rows, LANES), I32)
        shift_by = words_rows.bit_length() - 1
        picks = []
        for slot in range(indices.shape[0]):
            index = indices[slot : slot + 1, lanes]
            value = lax.shift_left(jnp.ones_like(index), 4 * lax.shift_right_logical(index, shift_by))
            if extra is None:
                value = jnp.where(length[pl.ds(column, 1), :] > slot, value, 0)
            picks.append((index, value))
        if extra is not None:
            value = lax.shift_left(jnp.ones_like(extra), 4 * lax.shift_right_logical(extra, shift_by))
            picks.append((extra, value))
        for index, value in picks:
            low = jnp.bitwise_and(index, words_rows - 1)
            words = words + jnp.where(low == row_at, value, 0)
        inv_here = lax.rsqrt(deg[pl.ds(column, 1), :].astype(F32))
        for nibble in range(8):
            count = jnp.bitwise_and(lax.shift_right_logical(words, 4 * nibble), 15)
            span = slice(nibble * words_rows, (nibble + 1) * words_rows)
            tile = count.astype(F32) * (scale_col[span, :] * inv_here)
            target[span, lanes] = tile.astype(BF16)

    def fill_halo(column, carry):
        lanes = pl.ds(pl.multiple_of(column * LANES, LANES), LANES)
        fill(hal_t, column, halo // 8, hnbrs, None, hinv_col, lanes)
        return carry

    def fill_adj(column, carry):
        lanes = pl.ds(pl.multiple_of(column * LANES, LANES), LANES)
        own = lax.broadcasted_iota(I32, (1, LANES), 1) + column * LANES
        fill(adj_t, column, rows // 8, nbrs, own, inv_col, lanes)
        return carry

    columns = rows // LANES
    lax.fori_loop(0, columns, fill_halo, 0)

    ask_one.arrive()
    lane_group = lax.broadcasted_iota(I32, (size_dp * 8, group), 1) // per_peer
    turned = jnp.zeros((size_dp * 8, group), I32)
    for source in range(size_mp):
        shift = lax.rem(source - me_mp + size_mp, size_mp) * per_peer
        moved = pltpu.roll(ask_mid[source], shift, 1)
        turned = jnp.where(lane_group == source, moved, turned)
    for part in range(size_dp):
        ask_turn[part] = turned[part * 8 : part * 8 + 8, :]
    ask_two.start()

    loads["up"].wait()
    half = p_src.shape[2]
    for part in range(size_dp):
        message = dot(hal_t[part * group : (part + 1) * group, :], up[...]).astype(BF16)
        p_src[part] = message[:, 0:half]
        q_src[part] = message[:, half:]
    p_one.start()
    loads["nbrs"].wait()
    spread_out(inv_col, deg)

    ask_two.arrive()
    lane_at = lax.broadcasted_iota(I32, (group, LANES), 1)
    ask_cols = [jnp.broadcast_to(ask_fin[part, 0:1, :], (LANES, group)).T for part in range(size_dp)]
    for part in range(size_dp):
        ask_col_ref[part * group : (part + 1) * group, :] = ask_cols[part]

    def fill_sel(column, carry):
        lanes = pl.ds(pl.multiple_of(column * LANES, LANES), LANES)
        here = lane_at + column * LANES
        for part in range(size_dp):
            span = slice(part * group, (part + 1) * group)
            sel[span, lanes] = jnp.where(ask_col_ref[span, :] == here, 1.0, 0.0).astype(BF16)
        return carry

    lax.fori_loop(0, columns, fill_sel, 0)

    def pick(table, target):
        def body(part, carry):
            here = pl.ds(pl.multiple_of(part * group, group), group)
            target[part] = dot(sel[here, :], table[...]).astype(BF16)
            return carry

        lax.fori_loop(0, size_dp, body, 0)

    loads["feat"].wait()
    pick(feat_tab, x_src)
    x_one.start()
    loads["emb"].wait()
    pick(emb_tab, e_src)
    e_one.start()
    loads["gradt"].wait()
    pick(grad_tab, v_src)
    v_one.start()

    q_one.start()
    p_one.arrive()
    p_two.start()
    lax.fori_loop(0, columns // 4, fill_adj, 0)
    x_one.arrive()
    x_two.start()
    lax.fori_loop(columns // 4, columns // 2, fill_adj, 0)
    e_one.arrive()
    e_two.start()
    lax.fori_loop(columns // 2, columns, fill_adj, 0)
    v_one.arrive()
    v_two.start()
    q_one.arrive()
    q_two.start()

    chunks = rows // CHUNK

    def at_chunk(step):
        return pl.ds(pl.multiple_of(step * CHUNK, CHUNK), CHUNK)

    loads["feats"].wait()
    feats_t[...] = feats[...].T
    loads["w1"].wait()
    w1_t = w1[...].T
    x_two.arrive()
    hx_t = x_fin[...].reshape(halo, x_fin.shape[-1]).T

    def layer_one(step, carry):
        here = at_chunk(step)
        agg = (dot(feats_t[...], adj_t[:, here]) + dot(hx_t, hal_t[:, here])).astype(BF16)
        agg1_t[:, here] = agg
        pre = dot(w1_t, agg)
        sigma = jax.nn.sigmoid(pre)
        hid_t[:, here] = (pre * sigma).astype(BF16)
        dfac_t[:, here] = sigma * (1.0 + pre * (1.0 - sigma))
        return carry

    lax.fori_loop(0, chunks, layer_one, 0)

    def own_two(step, carry):
        here = at_chunk(step)
        own2_t[:, here] = dot(hid_t[...], adj_t[:, here])
        return carry

    lax.fori_loop(0, chunks, own_two, 0)

    def own_spread(step, carry):
        here = at_chunk(step)
        spread_own[here, :] = dot(adj_t[here, :], up[...])
        hal[here, :] = hal_t[:, here].T
        return carry


    e_two.arrive()
    he_t = e_fin[...].reshape(halo, e_fin.shape[-1]).T

    def layer_two(step, carry):
        here = at_chunk(step)
        agg2_t[:, here] = (own2_t[:, here] + dot(he_t, hal_t[:, here])).astype(BF16)
        return carry

    lax.fori_loop(0, chunks, layer_two, 0)
    part2 = t2_src.shape[1]
    for peer in range(size_mp):
        strip = agg2_t[peer * part2 : (peer + 1) * part2, :]
        t2_src[peer] = dot(strip, up[...]).astype(BF16)
    t2_one.start()
    loads["w2"].wait()

    def output(step, carry):
        here = at_chunk(step)
        out_buf[here, :] = dot(agg2_t[:, here], w2[...], TN).astype(BF16)
        return carry

    lax.fori_loop(0, chunks, own_spread, 0)
    lax.fori_loop(0, chunks, output, 0)

    def total(ref, count):
        value = ref[0].astype(F32)
        for at in range(1, count):
            value = value + ref[at].astype(F32)
        return value

    t2_one.arrive()
    t2_sum[...] = total(t2_mid, size_mp).astype(BF16)
    t2_two.start()

    v_two.arrive()
    term1[...] = jnp.zeros_like(term1)
    hv = v_fin[...].reshape(halo, v_fin.shape[-1])

    def backward(step, carry):
        here = at_chunk(step)
        spread = (spread_own[here, :] + dot(hal[here, :], hv)).astype(BF16)
        back = dot(w2[...], spread, NT)
        d_pre = (back * dfac_t[:, here]).astype(BF16)
        term1[...] += dot(agg1_t[:, here], d_pre, NT)
        return carry

    lax.fori_loop(0, chunks, backward, 0)
    part1 = t1_src.shape[1]
    for peer in range(size_mp):
        t1_src[peer] = term1[peer * part1 : (peer + 1) * part1, :].astype(BF16)
    t1_one.start()

    q_two.arrive()
    p_two.arrive()
    hp = p_fin[...].reshape(halo, half)
    hq = q_fin[...].reshape(halo, half)

    def owner_sum(step, carry):
        here = at_chunk(step)
        hgrad_buf[here, 0:half] = dot(sel[:, here], hp, TN).astype(BF16)
        hgrad_buf[here, half:] = dot(sel[:, here], hq, TN).astype(BF16)
        return carry

    lax.fori_loop(0, chunks // 2, owner_sum, 0)
    t2_two.arrive()
    t2_all[me_mp] = (total(t2_fin, size_dp) * factor).astype(BF16)
    gather_start(t2_three)
    t1_one.arrive()
    t1_sum[...] = total(t1_mid, size_mp).astype(BF16)
    t1_two.start()
    lax.fori_loop(chunks // 2, chunks, owner_sum, 0)
    t1_two.arrive()
    t1_all[me_mp] = (total(t1_fin, size_dp) * factor).astype(BF16)
    gather_start(t1_three)

    gather_arrive(t2_three)
    for peer in range(size_mp):
        g2_ref[peer * part2 : (peer + 1) * part2, :] = t2_all[peer].astype(F32)
    gather_arrive(t1_three)
    for peer in range(size_mp):
        g1_ref[peer * part1 : (peer + 1) * part1, :] = t1_all[peer].astype(F32)
    for hop in hops:
        hop.finish()


def local_kernel(
    node_feats,
    batch_deg,
    batch_nbrs,
    halo_nbrs,
    halo_len,
    halo_rows,
    halo_deg,
    feat_table,
    emb_table,
    grad_table,
    weight_one,
    weight_two,
    grad_out,
):
    size_dp = lax.axis_size("dp")
    size_mp = lax.axis_size("mp")
    rows, feat = node_feats.shape
    halo = halo_rows.shape[0]
    shard_rows = feat_table.shape[0]
    hid_in, hid = weight_two.shape
    per_peer = halo // (size_dp * size_mp)
    group = size_mp * per_peer
    lines, halo_lines = rows // LANES, halo // LANES
    factor = 1.0 / float(rows * size_dp * size_mp) ** 0.5
    any_spec = pl.BlockSpec(memory_space=pl.ANY)
    vmem_spec = pl.BlockSpec(memory_space=pltpu.VMEM)
    vmem = pltpu.VMEM
    part1, part2 = feat // size_mp, hid // size_mp

    def three(width):
        return [vmem((size_dp, group, width), BF16)] * 3

    def sums(part):
        return [
            vmem((size_mp, part, hid), BF16),
            vmem((size_mp, part, hid), BF16),
            vmem((part, hid), BF16),
            vmem((size_dp, part, hid), BF16),
            vmem((size_mp, part, hid), BF16),
        ]

    return pl.pallas_call(
        functools.partial(kernel, size_dp, size_mp, per_peer, factor),
        out_shape=(
            pltpu.VMEM((rows, hid), BF16),
            pltpu.VMEM((shard_rows, hid), BF16),
            pltpu.VMEM((feat, hid), F32),
            pltpu.VMEM((hid_in, hid), F32),
        ),
        in_specs=[any_spec] * 13,
        out_specs=(vmem_spec,) * 4,
        scratch_shapes=[
            vmem((batch_nbrs.shape[1], rows), I32),
            vmem((halo_nbrs.shape[1], rows), I32),
            vmem((lines, LANES), I32),
            vmem((lines, LANES), I32),
            vmem((halo_lines, LANES), I32),
            vmem((halo_lines, LANES), I32),
            vmem(node_feats.shape, BF16),
            vmem(feat_table.shape, BF16),
            vmem(emb_table.shape, BF16),
            vmem(grad_table.shape, BF16),
            vmem(weight_one.shape, BF16),
            vmem(weight_two.shape, BF16),
            vmem(grad_out.shape, BF16),
            vmem((size_dp * 8, group), I32),
            vmem((size_mp, size_dp * 8, group), I32),
            vmem((size_dp, 8, group), I32),
            vmem((size_dp, 8, group), I32),
            vmem((halo, LANES), I32),
            vmem((rows, LANES), F32),
            vmem((halo, LANES), F32),
            vmem((rows, rows), BF16),
            vmem((halo, rows), BF16),
            vmem((halo, shard_rows), BF16),
            *three(feat),
            *three(hid),
            *three(hid),
            *three(hid // 2),
            *three(hid // 2),
            vmem((feat, rows), BF16),
            vmem((feat, rows), BF16),
            vmem((hid, rows), BF16),
            vmem((hid, rows), F32),
            vmem((hid, rows), F32),
            vmem((hid, rows), BF16),
            vmem((rows, hid), F32),
            vmem((feat, hid), F32),
            vmem((rows, halo), BF16),
            *sums(part1),
            *sums(part2),
            pltpu.SemaphoreType.DMA((13,)),
            pltpu.SemaphoreType.DMA((18,)),
            pltpu.SemaphoreType.DMA((10, size_mp)),
            pltpu.SemaphoreType.DMA((10, size_mp)),
            pltpu.SemaphoreType.DMA((8, size_dp)),
            pltpu.SemaphoreType.DMA((8, size_dp)),
        ],
        compiler_params=pltpu.CompilerParams(
            collective_id=0, has_side_effects=True, vmem_limit_bytes=VMEM_MIB * 1024 * 1024
        ),
    )(
        batch_nbrs.T,
        halo_nbrs.T,
        batch_deg.reshape(lines, LANES),
        halo_len.reshape(lines, LANES),
        halo_deg.reshape(halo_lines, LANES),
        halo_rows.reshape(halo_lines, LANES),
        node_feats, feat_table, emb_table, grad_table, weight_one, weight_two, grad_out)


def matrices(batch_deg, batch_nbrs, halo_nbrs, halo_len, halo_deg):
    rows = batch_nbrs.shape[0]
    halo_count = halo_deg.shape[0]
    inv_batch = lax.rsqrt(batch_deg.astype(jnp.float32))
    inv_halo = lax.rsqrt(halo_deg.astype(jnp.float32))
    self_coef = 1.0 / batch_deg.astype(jnp.float32)
    row_index = jnp.arange(rows, dtype=jnp.int32)
    halo_index = jnp.arange(halo_count, dtype=jnp.int32)
    counts = jnp.zeros((rows, rows), jnp.float32)
    for slot in range(batch_nbrs.shape[1]):
        counts = counts + (batch_nbrs[:, slot, None] == row_index[None, :]).astype(jnp.float32)
    halo_counts = jnp.zeros((rows, halo_count), jnp.float32)
    for slot in range(halo_nbrs.shape[1]):
        hit = (halo_nbrs[:, slot, None] == halo_index[None, :]) & (halo_len[:, None] > slot)
        halo_counts = halo_counts + hit.astype(jnp.float32)
    diagonal = jnp.where(
        row_index[:, None] == row_index[None, :], self_coef[:, None], jnp.float32(0.0)
    )
    adjacency = (counts * (inv_batch[:, None] * inv_batch[None, :]) + diagonal).astype(jnp.bfloat16)
    halo_mat = (halo_counts * (inv_batch[:, None] * inv_halo[None, :])).astype(jnp.bfloat16)
    return (adjacency, halo_mat)


def mult(left, right):
    return jnp.dot(left, right, preferred_element_type=jnp.float32)


def mult_t(left, right):
    return lax.dot_general(
        left, right, (((0,), (0,)), ((), ())), preferred_element_type=jnp.float32
    )


def local_plain(
    node_feats,
    batch_deg,
    batch_nbrs,
    halo_nbrs,
    halo_len,
    halo_rows,
    halo_deg,
    feat_table,
    emb_table,
    grad_table,
    weight_one,
    weight_two,
    grad_out,
):
    batch_rows = node_feats.shape[0]
    hidden_width = weight_two.shape[1]
    feat_width = feat_table.shape[1]
    size_dp = lax.axis_size("dp")
    size_mp = lax.axis_size("mp")
    devices = size_dp * size_mp
    halo_count = halo_rows.shape[0]
    per_peer = halo_count // devices
    shard_rows = feat_table.shape[0]
    offsets = halo_rows % shard_rows
    asked = lax.all_to_all(
        offsets.reshape(devices, per_peer), ("dp", "mp"), split_axis=0, concat_axis=0, tiled=True
    )
    shard_index = jnp.arange(shard_rows, dtype=jnp.int32)
    selector = (asked.reshape(-1)[:, None] == shard_index[None, :]).astype(jnp.bfloat16)
    lead = asked.shape
    picked_x = mult(selector, feat_table).astype(jnp.bfloat16).reshape(lead + (feat_width,))
    picked_e = mult(selector, emb_table).astype(jnp.bfloat16).reshape(lead + (hidden_width,))
    picked_v = mult(selector, grad_table).astype(jnp.bfloat16).reshape(lead + (hidden_width,))
    pulled = (
        lax.all_to_all(picked_x, ("dp", "mp"), split_axis=0, concat_axis=0, tiled=True),
        lax.all_to_all(picked_e, ("dp", "mp"), split_axis=0, concat_axis=0, tiled=True),
        lax.all_to_all(picked_v, ("dp", "mp"), split_axis=0, concat_axis=0, tiled=True),
    )
    halo_x = pulled[0].reshape(halo_count, feat_width)
    halo_e = pulled[1].reshape(halo_count, hidden_width)
    halo_v = pulled[2].reshape(halo_count, hidden_width)
    adjacency, halo_mat = matrices(batch_deg, batch_nbrs, halo_nbrs, halo_len, halo_deg)
    agg_one = (mult(adjacency, node_feats) + mult(halo_mat, halo_x)).astype(jnp.bfloat16)
    pre_one = mult(agg_one, weight_one)
    hidden = jax.nn.silu(pre_one).astype(jnp.bfloat16)
    agg_two = (mult(adjacency, hidden) + mult(halo_mat, halo_e)).astype(jnp.bfloat16)
    out_embed = mult(agg_two, weight_two).astype(jnp.bfloat16)
    partial_value = mult_t(halo_mat, grad_out)
    arrived = lax.all_to_all(
        partial_value.reshape(devices, per_peer, hidden_width),
        ("dp", "mp"),
        split_axis=0,
        concat_axis=0,
        tiled=True,
    )
    halo_grad = lax.dot_general(
        selector.astype(jnp.float32),
        arrived.reshape(-1, hidden_width),
        (((0,), (0,)), ((), ())),
        precision=lax.Precision.HIGHEST,
        preferred_element_type=jnp.float32,
    )
    halo_grad = halo_grad.astype(jnp.bfloat16)
    spread = (mult_t(adjacency, grad_out) + mult(halo_mat, halo_v)).astype(jnp.bfloat16)
    back_hidden = lax.dot_general(
        spread, weight_two, (((1,), (1,)), ((), ())), preferred_element_type=jnp.float32
    )
    sigma = jax.nn.sigmoid(pre_one)
    d_pre = (back_hidden * (sigma * (1.0 + pre_one * (1.0 - sigma)))).astype(jnp.bfloat16)
    term_two = mult_t(agg_two, grad_out)
    term_one = mult_t(agg_one, d_pre)
    column_sums = (
        lax.psum_scatter(term_one, "mp", scatter_dimension=1, tiled=True),
        lax.psum_scatter(term_two, "mp", scatter_dimension=1, tiled=True),
    )
    column_sums = lax.psum((column_sums[0], column_sums[1]), "dp")
    summed = (
        lax.all_gather(column_sums[0], "mp", axis=1, tiled=True),
        lax.all_gather(column_sums[1], "mp", axis=1, tiled=True),
    )
    factor = 1.0 / jnp.sqrt(jnp.float32(batch_rows * devices))
    return (out_embed, halo_grad, summed[0] * factor, summed[1] * factor)


def local(*args):
    size_dp, size_mp = lax.axis_size("dp"), lax.axis_size("mp")
    rows, halo = args[0].shape[0], args[5].shape[0]
    per_peer = halo // (size_dp * size_mp)
    if per_peer % 16 == 0 and size_mp * per_peer == LANES and rows == args[7].shape[0]:
        return local_kernel(*args)
    return local_plain(*args)


def solution(mesh):
    return jax.shard_map(
        local,
        mesh=mesh,
        in_specs=(
            P(("dp", "mp"), None),
            P(("dp", "mp")),
            P(("dp", "mp"), None),
            P(("dp", "mp"), None),
            P(("dp", "mp")),
            P(("dp", "mp")),
            P(("dp", "mp")),
            P(("dp", "mp"), None),
            P(("dp", "mp"), None),
            P(("dp", "mp"), None),
            P(),
            P(),
            P(("dp", "mp"), None),
        ),
        out_specs=(P(("dp", "mp"), None), P(("dp", "mp"), None), P(), P()),
        check_vma=False,
    )
```

```python
import functools

import jax
import jax.numpy as jnp
from jax import lax
from jax.experimental import pallas as pl
from jax.experimental.pallas import tpu as pltpu
from jax.sharding import PartitionSpec as P

F32 = jnp.float32
BF16 = jnp.bfloat16
I32 = jnp.int32
LANES = 128
CHUNK = 512
VMEM_MIB = 54
NN = (((1,), (0,)), ((), ()))
NT = (((1,), (1,)), ((), ()))
TN = (((0,), (0,)), ((), ()))


def dot(left, right, dims=NN):
    return lax.dot_general(left, right, dims, preferred_element_type=F32)


def kernel(
    size_dp,
    size_mp,
    per_peer,
    factor,
    nbrs_hbm,
    hnbrs_hbm,
    deg_hbm,
    len_hbm,
    hdeg_hbm,
    hrows_hbm,
    feats_hbm,
    feat_hbm,
    emb_hbm,
    gradt_hbm,
    w1_hbm,
    w2_hbm,
    up_hbm,
    out_buf,
    hgrad_buf,
    g1_ref,
    g2_ref,
    nbrs,
    hnbrs,
    deg,
    length,
    hdeg,
    hrows,
    feats,
    feat_tab,
    emb_tab,
    grad_tab,
    w1,
    w2,
    up,
    ask_src,
    ask_mid,
    ask_turn,
    ask_fin,
    ask_col_ref,
    inv_col,
    hinv_col,
    adj_t,
    hal_t,
    sel,
    x_src,
    x_mid,
    x_fin,
    e_src,
    e_mid,
    e_fin,
    v_src,
    v_mid,
    v_fin,
    p_src,
    p_mid,
    p_fin,
    q_src,
    q_mid,
    q_fin,
    feats_t,
    agg1_t,
    hid_t,
    dfac_t,
    own2_t,
    agg2_t,
    spread_own,
    term1,
    hal,
    t1_src,
    t1_mid,
    t1_sum,
    t1_fin,
    t1_all,
    t2_src,
    t2_mid,
    t2_sum,
    t2_fin,
    t2_all,
    load_sem,
    self_sem,
    send_mp,
    recv_mp,
    send_dp,
    recv_dp,
):
    me_dp = lax.axis_index("dp")
    me_mp = lax.axis_index("mp")
    rows = adj_t.shape[0]
    halo = hal_t.shape[0]
    group = size_mp * per_peer
    shard_rows = sel.shape[1]

    def load(at, source, target):
        return pltpu.make_async_copy(source, target, load_sem.at[at])

    loads = {
        "hrows": load(0, hrows_hbm, hrows),
        "nbrs": load(8, nbrs_hbm, nbrs),
        "hnbrs": load(9, hnbrs_hbm, hnbrs),
        "deg": load(10, deg_hbm, deg),
        "length": load(11, len_hbm, length),
        "hdeg": load(12, hdeg_hbm, hdeg),
        "emb": load(1, emb_hbm, emb_tab),
        "feat": load(2, feat_hbm, feat_tab),
        "gradt": load(3, gradt_hbm, grad_tab),
        "up": load(4, up_hbm, up),
        "feats": load(5, feats_hbm, feats),
        "w1": load(6, w1_hbm, w1),
        "w2": load(7, w2_hbm, w2),
    }
    for name in ("hrows", "deg", "hdeg", "length", "hnbrs", "nbrs", "up"):
        loads[name].start()
    for name in ("feat", "emb", "gradt", "feats", "w1", "w2"):
        loads[name].start()

    peers_mp = [lax.rem(me_mp + step, size_mp) for step in range(1, size_mp)]
    peers_dp = [lax.rem(me_dp + step, size_dp) for step in range(1, size_dp)]
    barrier = pltpu.get_barrier_semaphore()
    for peer in peers_mp:
        pl.semaphore_signal(barrier, inc=1, device_id=(me_dp, peer), device_id_type=pl.DeviceIdType.MESH)
    for peer in peers_dp:
        pl.semaphore_signal(barrier, inc=1, device_id=(peer, me_mp), device_id_type=pl.DeviceIdType.MESH)
    pl.semaphore_wait(barrier, size_mp - 1 + size_dp - 1)

    def to_mp(piece, peer, place, source, target):
        return pltpu.make_async_remote_copy(
            src_ref=source,
            dst_ref=target,
            send_sem=send_mp.at[piece, peer],
            recv_sem=recv_mp.at[piece, place],
            device_id=(me_dp, peer),
            device_id_type=pl.DeviceIdType.MESH,
        )

    def to_dp(piece, peer, place, source, target):
        return pltpu.make_async_remote_copy(
            src_ref=source,
            dst_ref=target,
            send_sem=send_dp.at[piece, peer],
            recv_sem=recv_dp.at[piece, place],
            device_id=(peer, me_mp),
            device_id_type=pl.DeviceIdType.MESH,
        )

    class Hop:
        def __init__(self, make, piece, me, peers, source_at, target_at, at):
            self.own = lambda: pltpu.make_async_copy(source_at(me), target_at(me), self_sem.at[at])
            self.out = [make(piece, peer, me, source_at(peer), target_at(me)) for peer in peers]
            self.come = [make(piece, peer, peer, source_at(peer), target_at(peer)) for peer in peers]

        def start(self):
            for copy in self.out:
                copy.start()
            self.own().start()

        def arrive(self):
            self.own().wait()
            for copy in self.come:
                copy.wait_recv()

        def finish(self):
            for copy in self.out:
                copy.wait_send()

    def block(ref, peer):
        return ref.at[:, pl.ds(pl.multiple_of(peer * per_peer, per_peer), per_peer), :]

    hops = []

    def hop_mp(piece, source_at, target_at):
        hop = Hop(to_mp, piece, me_mp, peers_mp, source_at, target_at, len(hops))
        hops.append(hop)
        return hop

    def hop_dp(piece, source_at, target_at):
        hop = Hop(to_dp, piece, me_dp, peers_dp, source_at, target_at, len(hops))
        hops.append(hop)
        return hop

    def swap(piece, source, middle, final):
        first = hop_mp(piece, lambda peer: block(source, peer), lambda peer: block(middle, peer))
        second = hop_dp(piece, lambda peer: middle.at[peer], lambda peer: final.at[peer])
        return first, second

    ask_one = hop_mp(0, lambda peer: ask_src, lambda peer: ask_mid.at[peer])
    ask_two = hop_dp(0, lambda peer: ask_turn.at[peer], lambda peer: ask_fin.at[peer])
    x_one, x_two = swap(1, x_src, x_mid, x_fin)
    e_one, e_two = swap(2, e_src, e_mid, e_fin)
    v_one, v_two = swap(3, v_src, v_mid, v_fin)
    p_one, p_two = swap(4, p_src, p_mid, p_fin)
    q_one, q_two = swap(7, q_src, q_mid, q_fin)
    t2_one = hop_mp(5, lambda peer: t2_src.at[peer], lambda peer: t2_mid.at[peer])
    t2_two = hop_dp(5, lambda peer: t2_sum, lambda peer: t2_fin.at[peer])
    t1_one = hop_mp(6, lambda peer: t1_src.at[peer], lambda peer: t1_mid.at[peer])
    t1_two = hop_dp(6, lambda peer: t1_sum, lambda peer: t1_fin.at[peer])
    t2_three = hop_mp(8, lambda peer: t2_all.at[me_mp], lambda peer: t2_all.at[peer])
    t1_three = hop_mp(9, lambda peer: t1_all.at[me_mp], lambda peer: t1_all.at[peer])

    def gather_start(hop):
        for copy in hop.out:
            copy.start()

    def gather_arrive(hop):
        for copy in hop.come:
            copy.wait_recv()

    loads["hrows"].wait()
    for part in range(size_dp):
        offsets = lax.rem(hrows[part : part + 1, :], shard_rows)
        ask_src[part * 8 : part * 8 + 8, :] = jnp.broadcast_to(offsets, (8, group))
    ask_one.start()

    for name in ("deg", "hdeg", "length", "hnbrs"):
        loads[name].wait()

    def spread_out(target, source):
        for at in range(source.shape[0]):
            piece = lax.rsqrt(source[at : at + 1, :].astype(F32))
            target[at * LANES : (at + 1) * LANES, :] = jnp.broadcast_to(piece, (LANES, LANES)).T

    spread_out(hinv_col, hdeg)

    def fill(target, column, words_rows, indices, extra, scale_col, lanes):
        row_at = lax.broadcasted_iota(I32, (words_rows, LANES), 0)
        words = jnp.zeros((words_rows, LANES), I32)
        shift_by = words_rows.bit_length() - 1
        picks = []
        for slot in range(indices.shape[0]):
            index = indices[slot : slot + 1, lanes]
            value = lax.shift_left(jnp.ones_like(index), 4 * lax.shift_right_logical(index, shift_by))
            if extra is None:
                value = jnp.where(length[pl.ds(column, 1), :] > slot, value, 0)
            picks.append((index, value))
        if extra is not None:
            value = lax.shift_left(jnp.ones_like(extra), 4 * lax.shift_right_logical(extra, shift_by))
            picks.append((extra, value))
        for index, value in picks:
            low = jnp.bitwise_and(index, words_rows - 1)
            words = words + jnp.where(low == row_at, value, 0)
        inv_here = lax.rsqrt(deg[pl.ds(column, 1), :].astype(F32))
        for nibble in range(8):
            count = jnp.bitwise_and(lax.shift_right_logical(words, 4 * nibble), 15)
            span = slice(nibble * words_rows, (nibble + 1) * words_rows)
            tile = count.astype(F32) * (scale_col[span, :] * inv_here)
            target[span, lanes] = tile.astype(BF16)

    def fill_halo(column, carry):
        lanes = pl.ds(pl.multiple_of(column * LANES, LANES), LANES)
        fill(hal_t, column, halo // 8, hnbrs, None, hinv_col, lanes)
        return carry

    def fill_adj(column, carry):
        lanes = pl.ds(pl.multiple_of(column * LANES, LANES), LANES)
        own = lax.broadcasted_iota(I32, (1, LANES), 1) + column * LANES
        fill(adj_t, column, rows // 8, nbrs, own, inv_col, lanes)
        return carry

    columns = rows // LANES
    lax.fori_loop(0, columns, fill_halo, 0)

    ask_one.arrive()
    lane_group = lax.broadcasted_iota(I32, (size_dp * 8, group), 1) // per_peer
    turned = jnp.zeros((size_dp * 8, group), I32)
    for source in range(size_mp):
        shift = lax.rem(source - me_mp + size_mp, size_mp) * per_peer
        moved = pltpu.roll(ask_mid[source], shift, 1)
        turned = jnp.where(lane_group == source, moved, turned)
    for part in range(size_dp):
        ask_turn[part] = turned[part * 8 : part * 8 + 8, :]
    ask_two.start()

    loads["up"].wait()
    half = p_src.shape[2]
    message = dot(hal_t[...], up[...]).astype(BF16)
    p_src[...] = message[:, 0:half].reshape(p_src.shape)
    q_src[...] = message[:, half:].reshape(q_src.shape)
    p_one.start()
    loads["nbrs"].wait()
    spread_out(inv_col, deg)

    ask_two.arrive()
    lane_at = lax.broadcasted_iota(I32, (group, LANES), 1)
    ask_cols = [jnp.broadcast_to(ask_fin[part, 0:1, :], (LANES, group)).T for part in range(size_dp)]
    for part in range(size_dp):
        ask_col_ref[part * group : (part + 1) * group, :] = ask_cols[part]

    def fill_sel(column, carry):
        lanes = pl.ds(pl.multiple_of(column * LANES, LANES), LANES)
        here = lane_at + column * LANES
        for part in range(size_dp):
            span = slice(part * group, (part + 1) * group)
            sel[span, lanes] = jnp.where(ask_col_ref[span, :] == here, 1.0, 0.0).astype(BF16)
        return carry

    lax.fori_loop(0, columns, fill_sel, 0)

    def pick(table, target):
        target[...] = dot(sel[...], table[...]).astype(BF16).reshape(target.shape)

    loads["feat"].wait()
    pick(feat_tab, x_src)
    x_one.start()
    loads["emb"].wait()
    pick(emb_tab, e_src)
    e_one.start()
    loads["gradt"].wait()
    pick(grad_tab, v_src)
    v_one.start()

    q_one.start()
    p_one.arrive()
    p_two.start()
    lax.fori_loop(0, columns // 4, fill_adj, 0)
    x_one.arrive()
    x_two.start()
    lax.fori_loop(columns // 4, columns // 2, fill_adj, 0)
    e_one.arrive()
    e_two.start()
    lax.fori_loop(columns // 2, columns, fill_adj, 0)
    v_one.arrive()
    v_two.start()
    q_one.arrive()
    q_two.start()

    chunks = rows // CHUNK

    def at_chunk(step):
        return pl.ds(pl.multiple_of(step * CHUNK, CHUNK), CHUNK)

    loads["feats"].wait()
    feats_t[...] = feats[...].T
    loads["w1"].wait()
    w1_t = w1[...].T
    x_two.arrive()
    hx_t = x_fin[...].reshape(halo, x_fin.shape[-1]).T

    def layer_one(step, carry):
        here = at_chunk(step)
        agg = (dot(feats_t[...], adj_t[:, here]) + dot(hx_t, hal_t[:, here])).astype(BF16)
        agg1_t[:, here] = agg
        pre = dot(w1_t, agg)
        sigma = jax.nn.sigmoid(pre)
        hid_t[:, here] = (pre * sigma).astype(BF16)
        dfac_t[:, here] = sigma * (1.0 + pre * (1.0 - sigma))
        return carry

    lax.fori_loop(0, chunks, layer_one, 0)

    def own_two(step, carry):
        here = at_chunk(step)
        own2_t[:, here] = dot(hid_t[...], adj_t[:, here])
        return carry

    lax.fori_loop(0, chunks, own_two, 0)

    def own_spread(step, carry):
        here = pl.ds(pl.multiple_of(step * 2 * CHUNK, 2 * CHUNK), 2 * CHUNK)
        spread_own[here, :] = dot(adj_t[here, :], up[...])
        hal[here, :] = hal_t[:, here].T
        return carry


    e_two.arrive()
    he_t = e_fin[...].reshape(halo, e_fin.shape[-1]).T

    def layer_two(step, carry):
        here = at_chunk(step)
        agg2_t[:, here] = (own2_t[:, here] + dot(he_t, hal_t[:, here])).astype(BF16)
        return carry

    lax.fori_loop(0, chunks, layer_two, 0)
    part2 = t2_src.shape[1]
    t2_src[...] = dot(agg2_t[...], up[...]).astype(BF16).reshape(t2_src.shape)
    t2_one.start()
    loads["w2"].wait()

    def output(step, carry):
        here = at_chunk(step)
        out_buf[here, :] = dot(agg2_t[:, here], w2[...], TN).astype(BF16)
        return carry

    lax.fori_loop(0, chunks // 2, own_spread, 0)
    lax.fori_loop(0, chunks, output, 0)

    def total(ref, count):
        value = ref[0].astype(F32)
        for at in range(1, count):
            value = value + ref[at].astype(F32)
        return value

    t2_one.arrive()
    t2_sum[...] = total(t2_mid, size_mp).astype(BF16)
    t2_two.start()

    v_two.arrive()
    term1[...] = jnp.zeros_like(term1)
    hv = v_fin[...].reshape(halo, v_fin.shape[-1])

    def backward(step, carry):
        here = at_chunk(step)
        spread = (spread_own[here, :] + dot(hal[here, :], hv)).astype(BF16)
        back = dot(w2[...], spread, NT)
        d_pre = (back * dfac_t[:, here]).astype(BF16)
        term1[...] += dot(agg1_t[:, here], d_pre, NT)
        return carry

    lax.fori_loop(0, chunks, backward, 0)
    part1 = t1_src.shape[1]
    for peer in range(size_mp):
        t1_src[peer] = term1[peer * part1 : (peer + 1) * part1, :].astype(BF16)
    t1_one.start()

    q_two.arrive()
    p_two.arrive()
    arrived = jnp.concatenate(
        [p_fin[...].reshape(halo, half), q_fin[...].reshape(halo, half)], axis=1
    )

    def owner_sum(step, carry):
        here = at_chunk(step)
        hgrad_buf[here, :] = dot(sel[:, here], arrived, TN).astype(BF16)
        return carry

    lax.fori_loop(0, chunks // 2, owner_sum, 0)
    t2_two.arrive()
    t2_all[me_mp] = (total(t2_fin, size_dp) * factor).astype(BF16)
    gather_start(t2_three)
    t1_one.arrive()
    t1_sum[...] = total(t1_mid, size_mp).astype(BF16)
    t1_two.start()
    lax.fori_loop(chunks // 2, chunks, owner_sum, 0)
    t1_two.arrive()
    t1_all[me_mp] = (total(t1_fin, size_dp) * factor).astype(BF16)
    gather_start(t1_three)

    gather_arrive(t2_three)
    for peer in range(size_mp):
        g2_ref[peer * part2 : (peer + 1) * part2, :] = t2_all[peer].astype(F32)
    gather_arrive(t1_three)
    for peer in range(size_mp):
        g1_ref[peer * part1 : (peer + 1) * part1, :] = t1_all[peer].astype(F32)
    for hop in hops:
        hop.finish()


def local_kernel(
    node_feats,
    batch_deg,
    batch_nbrs,
    halo_nbrs,
    halo_len,
    halo_rows,
    halo_deg,
    feat_table,
    emb_table,
    grad_table,
    weight_one,
    weight_two,
    grad_out,
):
    size_dp = lax.axis_size("dp")
    size_mp = lax.axis_size("mp")
    rows, feat = node_feats.shape
    halo = halo_rows.shape[0]
    shard_rows = feat_table.shape[0]
    hid_in, hid = weight_two.shape
    per_peer = halo // (size_dp * size_mp)
    group = size_mp * per_peer
    lines, halo_lines = rows // LANES, halo // LANES
    factor = 1.0 / float(rows * size_dp * size_mp) ** 0.5
    any_spec = pl.BlockSpec(memory_space=pl.ANY)
    vmem_spec = pl.BlockSpec(memory_space=pltpu.VMEM)
    vmem = pltpu.VMEM
    part1, part2 = feat // size_mp, hid // size_mp

    def three(width):
        return [vmem((size_dp, group, width), BF16)] * 3

    def sums(part):
        return [
            vmem((size_mp, part, hid), BF16),
            vmem((size_mp, part, hid), BF16),
            vmem((part, hid), BF16),
            vmem((size_dp, part, hid), BF16),
            vmem((size_mp, part, hid), BF16),
        ]

    return pl.pallas_call(
        functools.partial(kernel, size_dp, size_mp, per_peer, factor),
        out_shape=(
            pltpu.VMEM((rows, hid), BF16),
            pltpu.VMEM((shard_rows, hid), BF16),
            pltpu.VMEM((feat, hid), F32),
            pltpu.VMEM((hid_in, hid), F32),
        ),
        in_specs=[any_spec] * 13,
        out_specs=(vmem_spec,) * 4,
        scratch_shapes=[
            vmem((batch_nbrs.shape[1], rows), I32),
            vmem((halo_nbrs.shape[1], rows), I32),
            vmem((lines, LANES), I32),
            vmem((lines, LANES), I32),
            vmem((halo_lines, LANES), I32),
            vmem((halo_lines, LANES), I32),
            vmem(node_feats.shape, BF16),
            vmem(feat_table.shape, BF16),
            vmem(emb_table.shape, BF16),
            vmem(grad_table.shape, BF16),
            vmem(weight_one.shape, BF16),
            vmem(weight_two.shape, BF16),
            vmem(grad_out.shape, BF16),
            vmem((size_dp * 8, group), I32),
            vmem((size_mp, size_dp * 8, group), I32),
            vmem((size_dp, 8, group), I32),
            vmem((size_dp, 8, group), I32),
            vmem((halo, LANES), I32),
            vmem((rows, LANES), F32),
            vmem((halo, LANES), F32),
            vmem((rows, rows), BF16),
            vmem((halo, rows), BF16),
            vmem((halo, shard_rows), BF16),
            *three(feat),
            *three(hid),
            *three(hid),
            *three(hid // 2),
            *three(hid // 2),
            vmem((feat, rows), BF16),
            vmem((feat, rows), BF16),
            vmem((hid, rows), BF16),
            vmem((hid, rows), F32),
            vmem((hid, rows), F32),
            vmem((hid, rows), BF16),
            vmem((rows, hid), F32),
            vmem((feat, hid), F32),
            vmem((rows, halo), BF16),
            *sums(part1),
            *sums(part2),
            pltpu.SemaphoreType.DMA((13,)),
            pltpu.SemaphoreType.DMA((18,)),
            pltpu.SemaphoreType.DMA((10, size_mp)),
            pltpu.SemaphoreType.DMA((10, size_mp)),
            pltpu.SemaphoreType.DMA((8, size_dp)),
            pltpu.SemaphoreType.DMA((8, size_dp)),
        ],
        compiler_params=pltpu.CompilerParams(
            collective_id=0, has_side_effects=True, vmem_limit_bytes=VMEM_MIB * 1024 * 1024
        ),
    )(
        batch_nbrs.T,
        halo_nbrs.T,
        batch_deg.reshape(lines, LANES),
        halo_len.reshape(lines, LANES),
        halo_deg.reshape(halo_lines, LANES),
        halo_rows.reshape(halo_lines, LANES),
        node_feats, feat_table, emb_table, grad_table, weight_one, weight_two, grad_out)


def matrices(batch_deg, batch_nbrs, halo_nbrs, halo_len, halo_deg):
    rows = batch_nbrs.shape[0]
    halo_count = halo_deg.shape[0]
    inv_batch = lax.rsqrt(batch_deg.astype(jnp.float32))
    inv_halo = lax.rsqrt(halo_deg.astype(jnp.float32))
    self_coef = 1.0 / batch_deg.astype(jnp.float32)
    row_index = jnp.arange(rows, dtype=jnp.int32)
    halo_index = jnp.arange(halo_count, dtype=jnp.int32)
    counts = jnp.zeros((rows, rows), jnp.float32)
    for slot in range(batch_nbrs.shape[1]):
        counts = counts + (batch_nbrs[:, slot, None] == row_index[None, :]).astype(jnp.float32)
    halo_counts = jnp.zeros((rows, halo_count), jnp.float32)
    for slot in range(halo_nbrs.shape[1]):
        hit = (halo_nbrs[:, slot, None] == halo_index[None, :]) & (halo_len[:, None] > slot)
        halo_counts = halo_counts + hit.astype(jnp.float32)
    diagonal = jnp.where(
        row_index[:, None] == row_index[None, :], self_coef[:, None], jnp.float32(0.0)
    )
    adjacency = (counts * (inv_batch[:, None] * inv_batch[None, :]) + diagonal).astype(jnp.bfloat16)
    halo_mat = (halo_counts * (inv_batch[:, None] * inv_halo[None, :])).astype(jnp.bfloat16)
    return (adjacency, halo_mat)


def mult(left, right):
    return jnp.dot(left, right, preferred_element_type=jnp.float32)


def mult_t(left, right):
    return lax.dot_general(
        left, right, (((0,), (0,)), ((), ())), preferred_element_type=jnp.float32
    )


def local_plain(
    node_feats,
    batch_deg,
    batch_nbrs,
    halo_nbrs,
    halo_len,
    halo_rows,
    halo_deg,
    feat_table,
    emb_table,
    grad_table,
    weight_one,
    weight_two,
    grad_out,
):
    batch_rows = node_feats.shape[0]
    hidden_width = weight_two.shape[1]
    feat_width = feat_table.shape[1]
    size_dp = lax.axis_size("dp")
    size_mp = lax.axis_size("mp")
    devices = size_dp * size_mp
    halo_count = halo_rows.shape[0]
    per_peer = halo_count // devices
    shard_rows = feat_table.shape[0]
    offsets = halo_rows % shard_rows
    asked = lax.all_to_all(
        offsets.reshape(devices, per_peer), ("dp", "mp"), split_axis=0, concat_axis=0, tiled=True
    )
    shard_index = jnp.arange(shard_rows, dtype=jnp.int32)
    selector = (asked.reshape(-1)[:, None] == shard_index[None, :]).astype(jnp.bfloat16)
    lead = asked.shape
    picked_x = mult(selector, feat_table).astype(jnp.bfloat16).reshape(lead + (feat_width,))
    picked_e = mult(selector, emb_table).astype(jnp.bfloat16).reshape(lead + (hidden_width,))
    picked_v = mult(selector, grad_table).astype(jnp.bfloat16).reshape(lead + (hidden_width,))
    pulled = (
        lax.all_to_all(picked_x, ("dp", "mp"), split_axis=0, concat_axis=0, tiled=True),
        lax.all_to_all(picked_e, ("dp", "mp"), split_axis=0, concat_axis=0, tiled=True),
        lax.all_to_all(picked_v, ("dp", "mp"), split_axis=0, concat_axis=0, tiled=True),
    )
    halo_x = pulled[0].reshape(halo_count, feat_width)
    halo_e = pulled[1].reshape(halo_count, hidden_width)
    halo_v = pulled[2].reshape(halo_count, hidden_width)
    adjacency, halo_mat = matrices(batch_deg, batch_nbrs, halo_nbrs, halo_len, halo_deg)
    agg_one = (mult(adjacency, node_feats) + mult(halo_mat, halo_x)).astype(jnp.bfloat16)
    pre_one = mult(agg_one, weight_one)
    hidden = jax.nn.silu(pre_one).astype(jnp.bfloat16)
    agg_two = (mult(adjacency, hidden) + mult(halo_mat, halo_e)).astype(jnp.bfloat16)
    out_embed = mult(agg_two, weight_two).astype(jnp.bfloat16)
    partial_value = mult_t(halo_mat, grad_out)
    arrived = lax.all_to_all(
        partial_value.reshape(devices, per_peer, hidden_width),
        ("dp", "mp"),
        split_axis=0,
        concat_axis=0,
        tiled=True,
    )
    halo_grad = lax.dot_general(
        selector.astype(jnp.float32),
        arrived.reshape(-1, hidden_width),
        (((0,), (0,)), ((), ())),
        precision=lax.Precision.HIGHEST,
        preferred_element_type=jnp.float32,
    )
    halo_grad = halo_grad.astype(jnp.bfloat16)
    spread = (mult_t(adjacency, grad_out) + mult(halo_mat, halo_v)).astype(jnp.bfloat16)
    back_hidden = lax.dot_general(
        spread, weight_two, (((1,), (1,)), ((), ())), preferred_element_type=jnp.float32
    )
    sigma = jax.nn.sigmoid(pre_one)
    d_pre = (back_hidden * (sigma * (1.0 + pre_one * (1.0 - sigma)))).astype(jnp.bfloat16)
    term_two = mult_t(agg_two, grad_out)
    term_one = mult_t(agg_one, d_pre)
    column_sums = (
        lax.psum_scatter(term_one, "mp", scatter_dimension=1, tiled=True),
        lax.psum_scatter(term_two, "mp", scatter_dimension=1, tiled=True),
    )
    column_sums = lax.psum((column_sums[0], column_sums[1]), "dp")
    summed = (
        lax.all_gather(column_sums[0], "mp", axis=1, tiled=True),
        lax.all_gather(column_sums[1], "mp", axis=1, tiled=True),
    )
    factor = 1.0 / jnp.sqrt(jnp.float32(batch_rows * devices))
    return (out_embed, halo_grad, summed[0] * factor, summed[1] * factor)


def local(*args):
    size_dp, size_mp = lax.axis_size("dp"), lax.axis_size("mp")
    rows, halo = args[0].shape[0], args[5].shape[0]
    per_peer = halo // (size_dp * size_mp)
    if per_peer % 16 == 0 and size_mp * per_peer == LANES and rows == args[7].shape[0]:
        return local_kernel(*args)
    return local_plain(*args)


def solution(mesh):
    return jax.shard_map(
        local,
        mesh=mesh,
        in_specs=(
            P(("dp", "mp"), None),
            P(("dp", "mp")),
            P(("dp", "mp"), None),
            P(("dp", "mp"), None),
            P(("dp", "mp")),
            P(("dp", "mp")),
            P(("dp", "mp")),
            P(("dp", "mp"), None),
            P(("dp", "mp"), None),
            P(("dp", "mp"), None),
            P(),
            P(),
            P(("dp", "mp"), None),
        ),
        out_specs=(P(("dp", "mp"), None), P(("dp", "mp"), None), P(), P()),
        check_vma=False,
    )
```
